32 devices in a mesh: dp: 4 (over x, core), tensor: 8 (over z, y).
Axes of the slice: x: 2, y: 2, z: 4, core: 2. Of those that a mesh axis runs over, the one named last changes fastest.
Arguments:
- tokens: bfloat16 [64, 2560], P(('dp', 'tensor')), may hold values from -6 to 6
- cotangent: bfloat16 [64, 2560], P(('dp', 'tensor')), may hold values from -6 to 6
- gate_weight: bfloat16 [2560, 12800], P('dp', 'tensor'), may hold values from -0.125 to 0.125
- up_weight: bfloat16 [2560, 12800], P('dp', 'tensor'), may hold values from -0.125 to 0.125
- down_weight: bfloat16 [12800, 2560], P('tensor', 'dp'), may hold values from -0.0546875 to 0.0546875
Outputs:
- input_grad: bfloat16 [64, 2560], P(('dp', 'tensor'))
- grad_gate: bfloat16 [2560, 12800], P('dp', 'tensor')
- grad_up: bfloat16 [2560, 12800], P('dp', 'tensor')
- grad_down: bfloat16 [12800, 2560], P('tensor', 'dp')
The draws below stay inside these ranges and needn't reach their ends.
All inputs are finite; a program needn't handle non-finite values.
Results may differ from the reference program's by a relative error of at most 0.017.
Values may be sent and summed in bfloat16 or wider, within the bound.
No kernel may reach another device: no remote copies, remote signals or barrier semaphores. Data moves between devices by JAX's collectives and lax.ppermute only.
A program may use at most 128 MiB of HBM per device.

```python
import jax
import jax.numpy as jnp
from jax import lax

D = 2560
FF = 12800
GROUP = 16
TOKENS = 64
N_DP = 4


def shard_levels(key, shape, cuts, least, high):
    factor_of, own = 1.0, jax.random.fold_in(key, 6)
    for position, blocks in cuts:
        draws = jnp.exp(jax.random.uniform(jax.random.fold_in(own, position), (blocks,), jnp.float32, least / len(cuts), high / len(cuts)))
        factor_of = factor_of * jnp.repeat(draws, shape[position] // blocks).reshape([-1 if axis == position else 1 for axis in range(len(shape))])
    return factor_of


def centred(key, shape, deviation, limit, shards=(), dtype=jnp.bfloat16):
    entries = deviation * jax.random.normal(key, shape, jnp.float32)
    if shards:
        entries = entries * shard_levels(key, shape, shards, -0.22, 0.18)
    return jnp.clip(entries, -limit, limit).astype(dtype)


def setup_inputs(seed: int = 0) -> dict:
    key_list = jax.random.split(jax.random.key(seed), 6)
    tokens = centred(key_list[0], (TOKENS, D), 1.0, 6.0, ((0, 32),))
    cotangent = centred(key_list[1], (TOKENS, D), 1.0, 6.0, ((0, 32),))
    gate_weight = centred(key_list[2], (D, FF), D ** -0.5, 0.125, ((0, 4), (1, 8)))
    up_weight = centred(key_list[3], (D, FF), D ** -0.5, 0.125, ((0, 4), (1, 8)))
    down_weight = centred(key_list[4], (FF, D), FF ** -0.5, 0.0546875, ((0, 8), (1, 4)))
    return dict(tokens=tokens, cotangent=cotangent, gate_weight=gate_weight, up_weight=up_weight, down_weight=down_weight)


def reference(tokens, cotangent, gate_weight, up_weight, down_weight):
    gate = jnp.dot(tokens, gate_weight, preferred_element_type=jnp.float32)
    up = jnp.dot(tokens, up_weight, preferred_element_type=jnp.float32)
    sig = jax.nn.sigmoid(gate)
    hidden = (gate * sig * up).astype(jnp.bfloat16)
    hidden_grad = jnp.dot(cotangent, down_weight.T, preferred_element_type=jnp.float32)
    up_grad = (hidden_grad * gate * sig).astype(jnp.bfloat16)
    gate_grad = (hidden_grad * up * sig * (1.0 + gate * (1.0 - sig))).astype(jnp.bfloat16)
    input_grad = jnp.dot(gate_grad, gate_weight.T, preferred_element_type=jnp.float32)
    input_grad = input_grad + jnp.dot(up_grad, up_weight.T, preferred_element_type=jnp.float32)
    input_grad = input_grad.astype(jnp.bfloat16)

    groups = TOKENS // GROUP
    tok_groups = tokens.reshape(groups, GROUP, D)
    cot_groups = cotangent.reshape(groups, GROUP, D)
    gg_groups = gate_grad.reshape(groups, GROUP, FF)
    ug_groups = up_grad.reshape(groups, GROUP, FF)
    hid_groups = hidden.reshape(groups, GROUP, FF)

    def rounded(value):
        narrow = lax.optimization_barrier(value.astype(jnp.bfloat16))
        return narrow.astype(jnp.float32)

    def add_group(carry, items):
        acc_gate, acc_up, acc_down = carry
        tok_g, cot_g, gg_g, ug_g, hid_g = items
        acc_gate = acc_gate + rounded(jnp.dot(tok_g.T, gg_g, preferred_element_type=jnp.float32))
        acc_up = acc_up + rounded(jnp.dot(tok_g.T, ug_g, preferred_element_type=jnp.float32))
        acc_down = acc_down + rounded(jnp.dot(hid_g.T, cot_g, preferred_element_type=jnp.float32))
        return (acc_gate, acc_up, acc_down), None

    start = (jnp.zeros((D, FF), jnp.float32), jnp.zeros((D, FF), jnp.float32), jnp.zeros((FF, D), jnp.float32))
    totals, unused = lax.scan(add_group, start, (tok_groups, cot_groups, gg_groups, ug_groups, hid_groups))
    grad_gate = (totals[0] / N_DP).astype(jnp.bfloat16)
    grad_up = (totals[1] / N_DP).astype(jnp.bfloat16)
    grad_down = (totals[2] / N_DP).astype(jnp.bfloat16)
    return input_grad, grad_gate, grad_up, grad_down
```

```python
import jax
import jax.numpy as jnp
from jax import lax
from jax.sharding import PartitionSpec as P

F32 = jnp.float32
BF16 = jnp.bfloat16


def swap_cores(value, n_dp):
    return lax.ppermute(value, "dp", [(i, i ^ 1) for i in range(n_dp)])


def local(tokens, cotangent, gate_weight, up_weight, down_weight):
    n_dp = lax.axis_size("dp")
    n_tensor = lax.axis_size("tensor")
    rows, width = tokens.shape
    depth, units = gate_weight.shape
    group = rows * n_tensor
    chips = n_dp // 2
    half = chips * group
    core = lax.rem(lax.axis_index("dp"), 2)

    joined = jnp.concatenate([tokens, cotangent], axis=0)
    slices = jnp.stack([joined[:, d * depth : (d + 1) * depth] for d in range(n_dp)])
    slices = jnp.broadcast_to(slices[:, None], (n_dp, n_tensor, 2 * rows, depth))
    both = lax.all_to_all(
        slices.reshape(n_dp * n_tensor, 2 * rows, depth), ("dp", "tensor"), split_axis=0, concat_axis=0, tiled=True
    )

    def by_core(value):
        value = value.reshape(chips, 2, group, depth)
        value = jnp.where(core == 0, value[:, ::-1], value)
        return value.transpose(1, 0, 2, 3).reshape(2 * half, depth)

    tok, cot = by_core(both[:, :rows]), by_core(both[:, rows:])

    gate_rows, up_rows = gate_weight.T, up_weight.T
    up_p = jnp.einsum("td,fd->tf", tok, up_rows, preferred_element_type=F32)
    tok_gate, up_p = lax.optimization_barrier((tok, up_p))
    gate_p = jnp.einsum("td,fd->tf", tok_gate, gate_rows, preferred_element_type=F32)
    cot, gate_p = lax.optimization_barrier((cot, gate_p))
    hid_p = jnp.einsum("td,fd->tf", cot, down_weight, preferred_element_type=F32)

    def sum_over_dp(partial):
        got = swap_cores(partial[:half].astype(BF16), n_dp)
        mine = (partial[half:] + got.astype(F32)).astype(BF16)
        total = mine.astype(F32)
        for shift in range(1, chips):
            got = lax.ppermute(mine, "dp", [(i, (i + 2 * shift) % n_dp) for i in range(n_dp)])
            total = total + got.astype(F32)
        return total

    gate, up, hidden_grad = sum_over_dp(gate_p), sum_over_dp(up_p), sum_over_dp(hid_p)

    sig = jax.nn.sigmoid(gate)
    hidden = (gate * sig * up).astype(BF16)
    up_grad = (hidden_grad * gate * sig).astype(BF16)
    gate_grad = (hidden_grad * up * sig * (1.0 + gate * (1.0 - sig))).astype(BF16)
    gate_grad, up_grad, hidden = (
        jnp.concatenate([swap_cores(value, n_dp), value], axis=0) for value in (gate_grad, up_grad, hidden)
    )

    total = jnp.einsum("tf,fd->td", gate_grad, gate_rows, preferred_element_type=F32)
    total = total + jnp.einsum("tf,fd->td", up_grad, up_rows, preferred_element_type=F32)
    shares = total.astype(BF16).reshape(2, chips, group, depth).transpose(1, 0, 2, 3)
    shares = jnp.where(core == 0, shares[:, ::-1], shares).reshape(n_dp * n_tensor, rows, depth)
    shares = lax.all_to_all(shares, ("dp", "tensor"), split_axis=0, concat_axis=0, tiled=True)
    shares = jnp.sum(shares.astype(F32).reshape(n_dp, n_tensor, rows, depth), axis=1)
    input_grad = shares.transpose(1, 0, 2).reshape(rows, width).astype(BF16)

    grad_gate = (jnp.einsum("td,tf->df", tok, gate_grad, preferred_element_type=F32) / n_dp).astype(BF16)
    grad_up = (jnp.einsum("td,tf->df", tok, up_grad, preferred_element_type=F32) / n_dp).astype(BF16)
    grad_down = (jnp.einsum("tf,td->fd", hidden, cot, preferred_element_type=F32) / n_dp).astype(BF16)
    return (input_grad, grad_gate, grad_up, grad_down)


def solution(mesh):
    return jax.shard_map(
        local,
        mesh=mesh,
        in_specs=(
            P(("dp", "tensor"), None),
            P(("dp", "tensor"), None),
            P("dp", "tensor"),
            P("dp", "tensor"),
            P("tensor", "dp"),
        ),
        out_specs=(
            P(("dp", "tensor"), None),
            P("dp", "tensor"),
            P("dp", "tensor"),
            P("tensor", "dp"),
        ),
        check_vma=False,
    )
```

```python
import jax
import jax.numpy as jnp
from jax import lax
from jax.sharding import PartitionSpec as P

F32 = jnp.float32
BF16 = jnp.bfloat16


def swap_cores(value, n_dp):
    return lax.ppermute(value, "dp", [(i, i ^ 1) for i in range(n_dp)])


def local(tokens, cotangent, gate_weight, up_weight, down_weight):
    n_dp = lax.axis_size("dp")
    n_tensor = lax.axis_size("tensor")
    rows, width = tokens.shape
    depth, units = gate_weight.shape
    group = rows * n_tensor
    chips = n_dp // 2
    half = chips * group
    core = lax.rem(lax.axis_index("dp"), 2)

    joined = jnp.concatenate([tokens, cotangent], axis=0)
    slices = jnp.stack([joined[:, d * depth : (d + 1) * depth] for d in range(n_dp)])
    slices = jnp.broadcast_to(slices[:, None], (n_dp, n_tensor, 2 * rows, depth))
    both = lax.all_to_all(
        slices.reshape(n_dp * n_tensor, 2 * rows, depth), ("dp", "tensor"), split_axis=0, concat_axis=0, tiled=True
    )

    def by_core(value):
        value = value.reshape(chips, 2, group, depth)
        value = jnp.where(core == 0, value[:, ::-1], value)
        return value.transpose(1, 0, 2, 3).reshape(2 * half, depth)

    tok, cot = by_core(both[:, :rows]), by_core(both[:, rows:])

    gate_rows, up_rows = gate_weight.T, up_weight.T

    def core_sum(partial):
        got = swap_cores(partial[:half].astype(BF16), n_dp)
        return (partial[half:] + got.astype(F32)).astype(BF16)

    def chip_sum(mine):
        total = mine.astype(F32)
        for shift in range(1, chips):
            got = lax.ppermute(mine, "dp", [(i, (i + 2 * shift) % n_dp) for i in range(n_dp)])
            total = total + got.astype(F32)
        return total

    up_p = jnp.einsum("td,fd->tf", tok, up_rows, preferred_element_type=F32)
    tok_gate, up_p = lax.optimization_barrier((tok, up_p))
    gate_p = jnp.einsum("td,fd->tf", tok_gate, gate_rows, preferred_element_type=F32)
    up, gate = core_sum(up_p), core_sum(gate_p)
    cot_hid, up = lax.optimization_barrier((cot, up))
    hid_p = jnp.einsum("td,fd->tf", cot_hid, down_weight, preferred_element_type=F32)
    up, gate, hidden_grad = chip_sum(up), chip_sum(gate), chip_sum(core_sum(hid_p))

    sig = jax.nn.sigmoid(gate)
    hidden = (gate * sig * up).astype(BF16)
    up_grad = (hidden_grad * gate * sig).astype(BF16)
    gate_grad = (hidden_grad * up * sig * (1.0 + gate * (1.0 - sig))).astype(BF16)
    gate_grad, up_grad, hidden = (
        jnp.concatenate([swap_cores(value, n_dp), value], axis=0) for value in (gate_grad, up_grad, hidden)
    )

    total = jnp.einsum("tf,fd->td", gate_grad, gate_rows, preferred_element_type=F32)
    total = total + jnp.einsum("tf,fd->td", up_grad, up_rows, preferred_element_type=F32)
    shares = total.astype(BF16).reshape(2, chips, group, depth).transpose(1, 0, 2, 3)
    shares = jnp.where(core == 0, shares[:, ::-1], shares).reshape(n_dp * n_tensor, rows, depth)
    shares = lax.all_to_all(shares, ("dp", "tensor"), split_axis=0, concat_axis=0, tiled=True)
    shares = jnp.sum(shares.astype(F32).reshape(n_dp, n_tensor, rows, depth), axis=1)
    input_grad = shares.transpose(1, 0, 2).reshape(rows, width).astype(BF16)

    grad_gate = (jnp.einsum("td,tf->df", tok, gate_grad, preferred_element_type=F32) / n_dp).astype(BF16)
    grad_up = (jnp.einsum("td,tf->df", tok, up_grad, preferred_element_type=F32) / n_dp).astype(BF16)
    grad_down = (jnp.einsum("tf,td->fd", hidden, cot, preferred_element_type=F32) / n_dp).astype(BF16)
    return (input_grad, grad_gate, grad_up, grad_down)


def solution(mesh):
    return jax.shard_map(
        local,
        mesh=mesh,
        in_specs=(
            P(("dp", "tensor"), None),
            P(("dp", "tensor"), None),
            P("dp", "tensor"),
            P("dp", "tensor"),
            P("tensor", "dp"),
        ),
        out_specs=(
            P(("dp", "tensor"), None),
            P("dp", "tensor"),
            P("dp", "tensor"),
            P("tensor", "dp"),
        ),
        check_vma=False,
    )
```

```python
import jax
import jax.numpy as jnp
from jax import lax
from jax.sharding import PartitionSpec as P

F32 = jnp.float32
BF16 = jnp.bfloat16


def swap_cores(value, n_dp):
    return lax.ppermute(value, "dp", [(i, i ^ 1) for i in range(n_dp)])


def local(tokens, cotangent, gate_weight, up_weight, down_weight):
    n_dp = lax.axis_size("dp")
    n_tensor = lax.axis_size("tensor")
    rows, width = tokens.shape
    depth, units = gate_weight.shape
    group = rows * n_tensor
    chips = n_dp // 2
    half = chips * group
    core = lax.rem(lax.axis_index("dp"), 2)

    joined = jnp.concatenate([tokens, cotangent], axis=0)
    slices = [joined[:, d * depth : (d + 1) * depth] for d in range(n_dp)]
    even, odd = jnp.stack(slices[0::2]), jnp.stack(slices[1::2])
    blocks = jnp.concatenate(
        [swap_cores(jnp.where(core == 0, odd, even), n_dp), jnp.where(core == 0, even, odd)], axis=1
    )
    blocks = jnp.broadcast_to(blocks[:, None], (chips, n_tensor, 4 * rows, depth))
    same_core = [
        [(2 * chip + c) * n_tensor + t for chip in range(chips) for t in range(n_tensor)] for c in range(2)
    ]
    both = lax.all_to_all(
        blocks.reshape(chips * n_tensor, 4 * rows, depth),
        ("dp", "tensor"),
        split_axis=0,
        concat_axis=0,
        axis_index_groups=same_core,
        tiled=True,
    )
    both = both.reshape(chips * n_tensor, 2, 2, rows, depth).transpose(2, 1, 0, 3, 4)
    tok, cot = both.reshape(2, 2 * half, depth)

    gate_rows, up_rows = gate_weight.T, up_weight.T

    def core_sum(partial):
        got = swap_cores(partial[:half].astype(BF16), n_dp)
        return (partial[half:] + got.astype(F32)).astype(BF16)

    def chip_sum(mine):
        total = mine.astype(F32)
        for shift in range(1, chips):
            got = lax.ppermute(mine, "dp", [(i, (i + 2 * shift) % n_dp) for i in range(n_dp)])
            total = total + got.astype(F32)
        return total

    up_p = jnp.einsum("td,fd->tf", tok, up_rows, preferred_element_type=F32)
    tok_gate, up_p = lax.optimization_barrier((tok, up_p))
    gate_p = jnp.einsum("td,fd->tf", tok_gate, gate_rows, preferred_element_type=F32)
    up, gate = core_sum(up_p), core_sum(gate_p)
    cot_hid, up = lax.optimization_barrier((cot, up))
    hid_p = jnp.einsum("td,fd->tf", cot_hid, down_weight, preferred_element_type=F32)
    up, gate, hidden_grad = chip_sum(up), chip_sum(gate), chip_sum(core_sum(hid_p))

    sig = jax.nn.sigmoid(gate)
    hidden = (gate * sig * up).astype(BF16)
    up_grad = (hidden_grad * gate * sig).astype(BF16)
    gate_grad = (hidden_grad * up * sig * (1.0 + gate * (1.0 - sig))).astype(BF16)
    gate_grad, up_grad, hidden = (
        jnp.concatenate([swap_cores(value, n_dp), value], axis=0) for value in (gate_grad, up_grad, hidden)
    )

    total = jnp.einsum("tf,fd->td", gate_grad, gate_rows, preferred_element_type=F32)
    total = total + jnp.einsum("tf,fd->td", up_grad, up_rows, preferred_element_type=F32)
    shares = total.astype(BF16).reshape(2, chips, group, depth).transpose(1, 0, 2, 3)
    shares = jnp.where(core == 0, shares[:, ::-1], shares).reshape(n_dp * n_tensor, rows, depth)
    shares = lax.all_to_all(shares, ("dp", "tensor"), split_axis=0, concat_axis=0, tiled=True)
    shares = jnp.sum(shares.astype(F32).reshape(n_dp, n_tensor, rows, depth), axis=1)
    input_grad = shares.transpose(1, 0, 2).reshape(rows, width).astype(BF16)

    grad_gate = (jnp.einsum("td,tf->df", tok, gate_grad, preferred_element_type=F32) / n_dp).astype(BF16)
    grad_up = (jnp.einsum("td,tf->df", tok, up_grad, preferred_element_type=F32) / n_dp).astype(BF16)
    grad_down = (jnp.einsum("tf,td->fd", hidden, cot, preferred_element_type=F32) / n_dp).astype(BF16)
    return (input_grad, grad_gate, grad_up, grad_down)


def solution(mesh):
    return jax.shard_map(
        local,
        mesh=mesh,
        in_specs=(
            P(("dp", "tensor"), None),
            P(("dp", "tensor"), None),
            P("dp", "tensor"),
            P("dp", "tensor"),
            P("tensor", "dp"),
        ),
        out_specs=(
            P(("dp", "tensor"), None),
            P("dp", "tensor"),
            P("dp", "tensor"),
            P("tensor", "dp"),
        ),
        check_vma=False,
    )
```

```python
import jax
import jax.numpy as jnp
from jax import lax
from jax.sharding import PartitionSpec as P

F32 = jnp.float32
BF16 = jnp.bfloat16


def swap_cores(value, n_dp):
    return lax.ppermute(value, "dp", [(i, i ^ 1) for i in range(n_dp)])


def local(tokens, cotangent, gate_weight, up_weight, down_weight):
    n_dp = lax.axis_size("dp")
    n_tensor = lax.axis_size("tensor")
    rows, width = tokens.shape
    depth, units = gate_weight.shape
    group = rows * n_tensor
    chips = n_dp // 2
    half = chips * group
    core = lax.rem(lax.axis_index("dp"), 2)

    joined = jnp.concatenate([tokens, cotangent], axis=0)
    slices = jnp.stack([joined[:, d * depth : (d + 1) * depth] for d in range(n_dp)])
    slices = jnp.broadcast_to(slices[:, None], (n_dp, n_tensor, 2 * rows, depth))
    both = lax.all_to_all(
        slices.reshape(n_dp * n_tensor, 2 * rows, depth), ("dp", "tensor"), split_axis=0, concat_axis=0, tiled=True
    )

    def by_core(value):
        value = value.reshape(chips, 2, group, depth)
        value = jnp.where(core == 0, value[:, ::-1], value)
        return value.transpose(1, 0, 2, 3).reshape(2 * half, depth)

    tok, cot = by_core(both[:, :rows]), by_core(both[:, rows:])

    gate_rows, up_rows = gate_weight.T, up_weight.T

    def core_sum(partial):
        got = swap_cores(partial[:half].astype(BF16), n_dp)
        return (partial[half:] + got.astype(F32)).astype(BF16)

    def chip_sum(mine):
        total = mine.astype(F32)
        for shift in range(1, chips):
            got = lax.ppermute(mine, "dp", [(i, (i + 2 * shift) % n_dp) for i in range(n_dp)])
            total = total + got.astype(F32)
        return total

    up_p = jnp.einsum("td,fd->tf", tok, up_rows, preferred_element_type=F32)
    up = core_sum(up_p)
    tok_gate, cot_hid, up = lax.optimization_barrier((tok, cot, up))
    gate_p = jnp.einsum("td,fd->tf", tok_gate, gate_rows, preferred_element_type=F32)
    gate = core_sum(gate_p)
    cot_hid, gate_p = lax.optimization_barrier((cot_hid, gate_p))
    hid_p = jnp.einsum("td,fd->tf", cot_hid, down_weight, preferred_element_type=F32)
    up, gate, hidden_grad = chip_sum(up), chip_sum(gate), chip_sum(core_sum(hid_p))

    sig = jax.nn.sigmoid(gate)
    hidden = (gate * sig * up).astype(BF16)
    up_grad = (hidden_grad * gate * sig).astype(BF16)
    gate_grad = (hidden_grad * up * sig * (1.0 + gate * (1.0 - sig))).astype(BF16)
    gate_grad, up_grad, hidden = (
        jnp.concatenate([swap_cores(value, n_dp), value], axis=0) for value in (gate_grad, up_grad, hidden)
    )

    total = jnp.einsum("tf,fd->td", gate_grad, gate_rows, preferred_element_type=F32)
    total = total + jnp.einsum("tf,fd->td", up_grad, up_rows, preferred_element_type=F32)
    shares = total.astype(BF16).reshape(2, chips, group, depth).transpose(1, 0, 2, 3)
    shares = jnp.where(core == 0, shares[:, ::-1], shares).reshape(n_dp * n_tensor, rows, depth)
    shares = lax.all_to_all(shares, ("dp", "tensor"), split_axis=0, concat_axis=0, tiled=True)
    shares = jnp.sum(shares.astype(F32).reshape(n_dp, n_tensor, rows, depth), axis=1)
    input_grad = shares.transpose(1, 0, 2).reshape(rows, width).astype(BF16)

    grad_gate = (jnp.einsum("td,tf->df", tok, gate_grad, preferred_element_type=F32) / n_dp).astype(BF16)
    grad_up = (jnp.einsum("td,tf->df", tok, up_grad, preferred_element_type=F32) / n_dp).astype(BF16)
    grad_down = (jnp.einsum("tf,td->fd", hidden, cot, preferred_element_type=F32) / n_dp).astype(BF16)
    return (input_grad, grad_gate, grad_up, grad_down)


def solution(mesh):
    return jax.shard_map(
        local,
        mesh=mesh,
        in_specs=(
            P(("dp", "tensor"), None),
            P(("dp", "tensor"), None),
            P("dp", "tensor"),
            P("dp", "tensor"),
            P("tensor", "dp"),
        ),
        out_specs=(
            P(("dp", "tensor"), None),
            P("dp", "tensor"),
            P("dp", "tensor"),
            P("tensor", "dp"),
        ),
        check_vma=False,
    )
```

```python
import jax
import jax.numpy as jnp
from jax import lax
from jax.sharding import PartitionSpec as P

F32 = jnp.float32
BF16 = jnp.bfloat16


def swap_cores(value, n_dp):
    return lax.ppermute(value, "dp", [(i, i ^ 1) for i in range(n_dp)])


def local(tokens, cotangent, gate_weight, up_weight, down_weight):
    n_dp = lax.axis_size("dp")
    n_tensor = lax.axis_size("tensor")
    rows, width = tokens.shape
    depth, units = gate_weight.shape
    group = rows * n_tensor
    chips = n_dp // 2
    half = chips * group
    core = lax.rem(lax.axis_index("dp"), 2)

    joined = jnp.concatenate([tokens, cotangent], axis=0)
    slices = jnp.stack([joined[:, d * depth : (d + 1) * depth] for d in range(n_dp)])
    slices = jnp.broadcast_to(slices[:, None], (n_dp, n_tensor, 2 * rows, depth))
    both = lax.all_to_all(
        slices.reshape(n_dp * n_tensor, 2 * rows, depth), ("dp", "tensor"), split_axis=0, concat_axis=0, tiled=True
    )

    def by_core(value):
        value = value.reshape(chips, 2, group, depth)
        value = jnp.where(core == 0, value[:, ::-1], value)
        return value.transpose(1, 0, 2, 3).reshape(2 * half, depth)

    tok, cot = by_core(both[:, :rows]), by_core(both[:, rows:])

    gate_rows, up_rows = gate_weight.T, up_weight.T

    def core_sum(partial):
        got = swap_cores(partial[:half].astype(BF16), n_dp)
        return (partial[half:] + got.astype(F32)).astype(BF16)

    def chip_sum(mine):
        total = mine.astype(F32)
        for shift in range(1, chips):
            got = lax.ppermute(mine, "dp", [(i, (i + 2 * shift) % n_dp) for i in range(n_dp)])
            total = total + got.astype(F32)
        return total

    hid_p = jnp.einsum("td,fd->tf", cot, down_weight, preferred_element_type=F32)
    tok_up, hid_p = lax.optimization_barrier((tok, hid_p))
    up_p = jnp.einsum("td,fd->tf", tok_up, up_rows, preferred_element_type=F32)
    hidden_grad, up = core_sum(hid_p), core_sum(up_p)
    tok_gate, hidden_grad = lax.optimization_barrier((tok, hidden_grad))
    gate_p = jnp.einsum("td,fd->tf", tok_gate, gate_rows, preferred_element_type=F32)
    hidden_grad, up, gate = chip_sum(hidden_grad), chip_sum(up), core_sum(gate_p)

    def both_cores(value):
        return jnp.concatenate([swap_cores(value, n_dp), value], axis=0)

    first = units // 256 * 128
    spans = [slice(0, first), slice(first, units)] if first else [slice(0, units)]
    packed, hidden = [], []
    for span in spans:
        part_gate, part_up, part_hid = chip_sum(gate[:, span]), up[:, span], hidden_grad[:, span]
        sig = jax.nn.sigmoid(part_gate)
        grads = [
            (part_hid * part_up * sig * (1.0 + part_gate * (1.0 - sig))).astype(BF16),
            (part_hid * part_gate * sig).astype(BF16),
        ]
        grads = jnp.concatenate(grads, axis=1)
        packed.append((swap_cores(grads, n_dp), grads))
        hidden.append((part_gate * sig * part_up).astype(BF16))
    hidden = jnp.concatenate(hidden, axis=1)
    total, parts = None, []
    for span, (other, own) in zip(spans, packed):
        if total is not None:
            total, other = lax.optimization_barrier((total, other))
        parts.append(jnp.split(jnp.concatenate([other, own], axis=0), 2, axis=1))
        part = jnp.einsum("tf,fd->td", parts[-1][0], gate_rows[span], preferred_element_type=F32)
        part = part + jnp.einsum("tf,fd->td", parts[-1][1], up_rows[span], preferred_element_type=F32)
        total = part if total is None else total + part
    gate_grad, up_grad = (jnp.concatenate(values, axis=1) for values in zip(*parts))
    shares = total.astype(BF16).reshape(2, chips, group, depth).transpose(1, 0, 2, 3)
    shares = jnp.where(core == 0, shares[:, ::-1], shares).reshape(n_dp * n_tensor, rows, depth)
    shares, tok, cot, hidden = lax.optimization_barrier((shares, tok, cot, hidden))
    hidden = both_cores(hidden)
    shares = lax.all_to_all(shares, ("dp", "tensor"), split_axis=0, concat_axis=0, tiled=True)
    shares = jnp.sum(shares.astype(F32).reshape(n_dp, n_tensor, rows, depth), axis=1)
    input_grad = shares.transpose(1, 0, 2).reshape(rows, width).astype(BF16)

    grad_gate = (jnp.einsum("td,tf->df", tok, gate_grad, preferred_element_type=F32) / n_dp).astype(BF16)
    grad_up = (jnp.einsum("td,tf->df", tok, up_grad, preferred_element_type=F32) / n_dp).astype(BF16)
    grad_down = (jnp.einsum("tf,td->fd", hidden, cot, preferred_element_type=F32) / n_dp).astype(BF16)
    return (input_grad, grad_gate, grad_up, grad_down)


def solution(mesh):
    return jax.shard_map(
        local,
        mesh=mesh,
        in_specs=(
            P(("dp", "tensor"), None),
            P(("dp", "tensor"), None),
            P("dp", "tensor"),
            P("dp", "tensor"),
            P("tensor", "dp"),
        ),
        out_specs=(
            P(("dp", "tensor"), None),
            P("dp", "tensor"),
            P("dp", "tensor"),
            P("tensor", "dp"),
        ),
        check_vma=False,
    )
```

```python
import jax
import jax.numpy as jnp
from jax import lax
from jax.sharding import PartitionSpec as P

F32 = jnp.float32
BF16 = jnp.bfloat16


def swap_cores(value, n_dp):
    return lax.ppermute(value, "dp", [(i, i ^ 1) for i in range(n_dp)])


def local(tokens, cotangent, gate_weight, up_weight, down_weight):
    n_dp = lax.axis_size("dp")
    n_tensor = lax.axis_size("tensor")
    rows, width = tokens.shape
    depth, units = gate_weight.shape
    group = rows * n_tensor
    chips = n_dp // 2
    half = chips * group
    core = lax.rem(lax.axis_index("dp"), 2)

    joined = jnp.concatenate([tokens, cotangent], axis=0)
    slices = jnp.stack([joined[:, d * depth : (d + 1) * depth] for d in range(n_dp)])
    slices = jnp.broadcast_to(slices[:, None], (n_dp, n_tensor, 2 * rows, depth))
    both = lax.all_to_all(
        slices.reshape(n_dp * n_tensor, 2 * rows, depth), ("dp", "tensor"), split_axis=0, concat_axis=0, tiled=True
    )

    def by_core(value):
        value = value.reshape(chips, 2, group, depth)
        value = jnp.where(core == 0, value[:, ::-1], value)
        return value.transpose(1, 0, 2, 3).reshape(2 * half, depth)

    tok, cot = by_core(both[:, :rows]), by_core(both[:, rows:])

    gate_rows, up_rows = gate_weight.T, up_weight.T

    def core_sum(partial):
        got = swap_cores(partial[:half].astype(BF16), n_dp)
        return (partial[half:] + got.astype(F32)).astype(BF16)

    def chip_sum(mine):
        total = mine.astype(F32)
        for shift in range(1, chips):
            got = lax.ppermute(mine, "dp", [(i, (i + 2 * shift) % n_dp) for i in range(n_dp)])
            total = total + got.astype(F32)
        return total

    hid_p = jnp.einsum("td,fd->tf", cot, down_weight, preferred_element_type=F32)
    tok_up, hid_p = lax.optimization_barrier((tok, hid_p))
    up_p = jnp.einsum("td,fd->tf", tok_up, up_rows, preferred_element_type=F32)
    hidden_grad, up = core_sum(hid_p), core_sum(up_p)
    tok_gate, hidden_grad = lax.optimization_barrier((tok, hidden_grad))
    gate_p = jnp.einsum("td,fd->tf", tok_gate, gate_rows, preferred_element_type=F32)
    hidden_grad, up, gate = chip_sum(hidden_grad), chip_sum(up), core_sum(gate_p)

    def both_cores(value):
        return jnp.concatenate([swap_cores(value, n_dp), value], axis=0)

    first = units // 256 * 128
    spans = [slice(0, first), slice(first, units)] if first else [slice(0, units)]
    packed, hidden = [], []
    for span in spans:
        part_gate, part_up, part_hid = chip_sum(gate[:, span]), up[:, span], hidden_grad[:, span]
        sig = jax.nn.sigmoid(part_gate)
        grads = [
            (part_hid * part_up * sig * (1.0 + part_gate * (1.0 - sig))).astype(BF16),
            (part_hid * part_gate * sig).astype(BF16),
        ]
        packed.append(([swap_cores(grad, n_dp) for grad in grads], grads))
        hidden.append((part_gate * sig * part_up).astype(BF16))
    hidden = jnp.concatenate(hidden, axis=1)
    total, parts = None, []
    for span, (other, own) in zip(spans, packed):
        if total is not None:
            total, other = lax.optimization_barrier((total, other))
        parts.append([jnp.concatenate(pair, axis=0) for pair in zip(other, own)])
        part = jnp.einsum("tf,fd->td", parts[-1][0], gate_rows[span], preferred_element_type=F32)
        part = part + jnp.einsum("tf,fd->td", parts[-1][1], up_rows[span], preferred_element_type=F32)
        total = part if total is None else total + part
    gate_grad, up_grad = (jnp.concatenate(values, axis=1) for values in zip(*parts))
    shares = total.astype(BF16).reshape(2, chips, group, depth).transpose(1, 0, 2, 3)
    shares = jnp.where(core == 0, shares[:, ::-1], shares).reshape(n_dp * n_tensor, rows, depth)
    shares, tok, cot, hidden = lax.optimization_barrier((shares, tok, cot, hidden))
    hidden = both_cores(hidden)
    shares = lax.all_to_all(shares, ("dp", "tensor"), split_axis=0, concat_axis=0, tiled=True)
    shares = jnp.sum(shares.astype(F32).reshape(n_dp, n_tensor, rows, depth), axis=1)
    input_grad = shares.transpose(1, 0, 2).reshape(rows, width).astype(BF16)

    grad_gate = (jnp.einsum("td,tf->df", tok, gate_grad, preferred_element_type=F32) / n_dp).astype(BF16)
    grad_up = (jnp.einsum("td,tf->df", tok, up_grad, preferred_element_type=F32) / n_dp).astype(BF16)
    grad_down = (jnp.einsum("tf,td->fd", hidden, cot, preferred_element_type=F32) / n_dp).astype(BF16)
    return (input_grad, grad_gate, grad_up, grad_down)


def solution(mesh):
    return jax.shard_map(
        local,
        mesh=mesh,
        in_specs=(
            P(("dp", "tensor"), None),
            P(("dp", "tensor"), None),
            P("dp", "tensor"),
            P("dp", "tensor"),
            P("tensor", "dp"),
        ),
        out_specs=(
            P(("dp", "tensor"), None),
            P("dp", "tensor"),
            P("dp", "tensor"),
            P("tensor", "dp"),
        ),
        check_vma=False,
    )
```

```python
import jax
import jax.numpy as jnp
from jax import lax
from jax.sharding import PartitionSpec as P

F32 = jnp.float32
BF16 = jnp.bfloat16


def swap_cores(value, n_dp):
    return lax.ppermute(value, "dp", [(i, i ^ 1) for i in range(n_dp)])


def local(tokens, cotangent, gate_weight, up_weight, down_weight):
    n_dp = lax.axis_size("dp")
    n_tensor = lax.axis_size("tensor")
    rows, width = tokens.shape
    depth, units = gate_weight.shape
    group = rows * n_tensor
    chips = n_dp // 2
    half = chips * group
    core = lax.rem(lax.axis_index("dp"), 2)

    joined = jnp.concatenate([tokens, cotangent], axis=0)
    slices = jnp.stack([joined[:, d * depth : (d + 1) * depth] for d in range(n_dp)])
    slices = jnp.broadcast_to(slices[:, None], (n_dp, n_tensor, 2 * rows, depth))
    both = lax.all_to_all(
        slices.reshape(n_dp * n_tensor, 2 * rows, depth), ("dp", "tensor"), split_axis=0, concat_axis=0, tiled=True
    )

    def by_core(value):
        value = value.reshape(chips, 2, group, depth)
        value = jnp.where(core == 0, value[:, ::-1], value)
        return value.transpose(1, 0, 2, 3).reshape(2 * half, depth)

    tok, cot = by_core(both[:, :rows]), by_core(both[:, rows:])

    gate_rows, up_rows = gate_weight.T, up_weight.T

    def core_sum(partial):
        got = swap_cores(partial[:half].astype(BF16), n_dp)
        return (partial[half:] + got.astype(F32)).astype(BF16)

    def chip_sum(mine):
        total = mine.astype(F32)
        for shift in range(1, chips):
            got = lax.ppermute(mine, "dp", [(i, (i + 2 * shift) % n_dp) for i in range(n_dp)])
            total = total + got.astype(F32)
        return total

    hid_p = jnp.einsum("td,fd->tf", cot, down_weight, preferred_element_type=F32)
    tok_up, hid_p = lax.optimization_barrier((tok, hid_p))
    up_p = jnp.einsum("td,fd->tf", tok_up, up_rows, preferred_element_type=F32)
    hidden_grad, up = core_sum(hid_p), core_sum(up_p)
    tok_gate, hidden_grad = lax.optimization_barrier((tok, hidden_grad))
    gate_p = jnp.einsum("td,fd->tf", tok_gate, gate_rows, preferred_element_type=F32)
    hidden_grad, up, gate = chip_sum(hidden_grad), chip_sum(up), core_sum(gate_p)

    def both_cores(value):
        return jnp.concatenate([swap_cores(value, n_dp), value], axis=0)

    first = units // 256 * 128
    spans = [slice(0, first), slice(first, units)] if first else [slice(0, units)]
    packed, hidden = [], []
    for span in spans:
        part_gate, part_up, part_hid = chip_sum(gate[:, span]), up[:, span], hidden_grad[:, span]
        sig = jax.nn.sigmoid(part_gate)
        grads = [
            (part_hid * part_up * sig * (1.0 + part_gate * (1.0 - sig))).astype(BF16),
            (part_hid * part_gate * sig).astype(BF16),
        ]
        if span.start:
            other = swap_cores(jnp.concatenate(grads, axis=0), n_dp)
            other = [other[:half], other[half:]]
        else:
            other = [swap_cores(grad, n_dp) for grad in grads]
        packed.append((other, grads))
        hidden.append((part_gate * sig * part_up).astype(BF16))
    hidden = jnp.concatenate(hidden, axis=1)
    total, parts = None, []
    for span, (other, own) in zip(spans, packed):
        if total is not None:
            total, other = lax.optimization_barrier((total, other))
        parts.append([jnp.concatenate(pair, axis=0) for pair in zip(other, own)])
        for grad, weight in zip(parts[-1], (gate_rows, up_rows)):
            part = jnp.einsum("tf,fd->td", grad, weight[span], preferred_element_type=F32)
            total = part if total is None else total + part
    gate_grad, up_grad = (jnp.concatenate(values, axis=1) for values in zip(*parts))
    shares = total.astype(BF16).reshape(2, chips, group, depth).transpose(1, 0, 2, 3)
    shares = jnp.where(core == 0, shares[:, ::-1], shares).reshape(n_dp * n_tensor, rows, depth)
    shares, tok, cot, hidden = lax.optimization_barrier((shares, tok, cot, hidden))
    hidden = both_cores(hidden)
    shares = lax.all_to_all(shares, ("dp", "tensor"), split_axis=0, concat_axis=0, tiled=True)
    shares = jnp.sum(shares.astype(F32).reshape(n_dp, n_tensor, rows, depth), axis=1)
    input_grad = shares.transpose(1, 0, 2).reshape(rows, width).astype(BF16)

    grad_gate = (jnp.einsum("td,tf->df", tok, gate_grad, preferred_element_type=F32) / n_dp).astype(BF16)
    grad_up = (jnp.einsum("td,tf->df", tok, up_grad, preferred_element_type=F32) / n_dp).astype(BF16)
    grad_down = (jnp.einsum("tf,td->fd", hidden, cot, preferred_element_type=F32) / n_dp).astype(BF16)
    return (input_grad, grad_gate, grad_up, grad_down)


def solution(mesh):
    return jax.shard_map(
        local,
        mesh=mesh,
        in_specs=(
            P(("dp", "tensor"), None),
            P(("dp", "tensor"), None),
            P("dp", "tensor"),
            P("dp", "tensor"),
            P("tensor", "dp"),
        ),
        out_specs=(
            P(("dp", "tensor"), None),
            P("dp", "tensor"),
            P("dp", "tensor"),
            P("tensor", "dp"),
        ),
        check_vma=False,
    )
```

```python
import jax
import jax.numpy as jnp
from jax import lax
from jax.sharding import PartitionSpec as P

F32 = jnp.float32
BF16 = jnp.bfloat16


def swap_cores(value, n_dp):
    return lax.ppermute(value, "dp", [(i, i ^ 1) for i in range(n_dp)])


def local(tokens, cotangent, gate_weight, up_weight, down_weight):
    n_dp = lax.axis_size("dp")
    n_tensor = lax.axis_size("tensor")
    rows, width = tokens.shape
    depth, units = gate_weight.shape
    group = rows * n_tensor
    chips = n_dp // 2
    half = chips * group
    core = lax.rem(lax.axis_index("dp"), 2)

    joined = jnp.concatenate([tokens, cotangent], axis=0)
    slices = jnp.stack([joined[:, d * depth : (d + 1) * depth] for d in range(n_dp)])
    slices = jnp.broadcast_to(slices[:, None], (n_dp, n_tensor, 2 * rows, depth))
    both = lax.all_to_all(
        slices.reshape(n_dp * n_tensor, 2 * rows, depth), ("dp", "tensor"), split_axis=0, concat_axis=0, tiled=True
    )

    def by_core(value):
        value = value.reshape(chips, 2, group, depth)
        value = jnp.where(core == 0, value[:, ::-1], value)
        return value.transpose(1, 0, 2, 3).reshape(2 * half, depth)

    cot = by_core(both[:, rows:])

    gate_rows, up_rows = gate_weight.T, up_weight.T

    def core_sum(partial):
        got = swap_cores(partial[:half].astype(BF16), n_dp)
        return (partial[half:] + got.astype(F32)).astype(BF16)

    def chip_sum(mine):
        total = mine.astype(F32)
        for shift in range(1, chips):
            got = lax.ppermute(mine, "dp", [(i, (i + 2 * shift) % n_dp) for i in range(n_dp)])
            total = total + got.astype(F32)
        return total

    hid_p = jnp.einsum("td,fd->tf", cot, down_weight, preferred_element_type=F32)
    both, hid_p = lax.optimization_barrier((both, hid_p))
    tok = by_core(both[:, :rows])
    up_p = jnp.einsum("td,fd->tf", tok, up_rows, preferred_element_type=F32)
    hidden_grad, up = core_sum(hid_p), core_sum(up_p)
    tok_gate, hidden_grad = lax.optimization_barrier((tok, hidden_grad))
    gate_p = jnp.einsum("td,fd->tf", tok_gate, gate_rows, preferred_element_type=F32)
    hidden_grad, up, gate = chip_sum(hidden_grad), chip_sum(up), core_sum(gate_p)

    def both_cores(value):
        return jnp.concatenate([swap_cores(value, n_dp), value], axis=0)

    first = units // 256 * 128
    spans = [slice(0, first), slice(first, units)] if first else [slice(0, units)]
    packed, hidden = [], []
    for span in spans:
        part_gate, part_up, part_hid = chip_sum(gate[:, span]), up[:, span], hidden_grad[:, span]
        sig = jax.nn.sigmoid(part_gate)
        grads = [
            (part_hid * part_up * sig * (1.0 + part_gate * (1.0 - sig))).astype(BF16),
            (part_hid * part_gate * sig).astype(BF16),
        ]
        packed.append(([swap_cores(grad, n_dp) for grad in grads], grads))
        hidden.append((part_gate * sig * part_up).astype(BF16))
    hidden = jnp.concatenate(hidden, axis=1)
    total, parts = None, []
    for span, (other, own) in zip(spans, packed):
        if total is not None:
            total, other = lax.optimization_barrier((total, other))
        parts.append([jnp.concatenate(pair, axis=0) for pair in zip(other, own)])
        part = jnp.einsum("tf,fd->td", parts[-1][0], gate_rows[span], preferred_element_type=F32)
        part = part + jnp.einsum("tf,fd->td", parts[-1][1], up_rows[span], preferred_element_type=F32)
        total = part if total is None else total + part
    gate_grad, up_grad = (jnp.concatenate(values, axis=1) for values in zip(*parts))
    shares = total.astype(BF16).reshape(2, chips, group, depth).transpose(1, 0, 2, 3)
    shares = jnp.where(core == 0, shares[:, ::-1], shares).reshape(n_dp * n_tensor, rows, depth)
    shares, tok, cot, hidden = lax.optimization_barrier((shares, tok, cot, hidden))
    hidden = both_cores(hidden)
    shares = lax.all_to_all(shares, ("dp", "tensor"), split_axis=0, concat_axis=0, tiled=True)
    shares = jnp.sum(shares.astype(F32).reshape(n_dp, n_tensor, rows, depth), axis=1)
    input_grad = shares.transpose(1, 0, 2).reshape(rows, width).astype(BF16)

    grad_gate = (jnp.einsum("td,tf->df", tok, gate_grad, preferred_element_type=F32) / n_dp).astype(BF16)
    grad_up = (jnp.einsum("td,tf->df", tok, up_grad, preferred_element_type=F32) / n_dp).astype(BF16)
    grad_down = (jnp.einsum("tf,td->fd", hidden, cot, preferred_element_type=F32) / n_dp).astype(BF16)
    return (input_grad, grad_gate, grad_up, grad_down)


def solution(mesh):
    return jax.shard_map(
        local,
        mesh=mesh,
        in_specs=(
            P(("dp", "tensor"), None),
            P(("dp", "tensor"), None),
            P("dp", "tensor"),
            P("dp", "tensor"),
            P("tensor", "dp"),
        ),
        out_specs=(
            P(("dp", "tensor"), None),
            P("dp", "tensor"),
            P("dp", "tensor"),
            P("tensor", "dp"),
        ),
        check_vma=False,
    )
```

```python
import jax
import jax.numpy as jnp
from jax import lax
from jax.sharding import PartitionSpec as P

F32 = jnp.float32
BF16 = jnp.bfloat16


def swap_cores(value, n_dp):
    return lax.ppermute(value, "dp", [(i, i ^ 1) for i in range(n_dp)])


def local(tokens, cotangent, gate_weight, up_weight, down_weight):
    n_dp = lax.axis_size("dp")
    n_tensor = lax.axis_size("tensor")
    rows, width = tokens.shape
    depth, units = gate_weight.shape
    group = rows * n_tensor
    chips = n_dp // 2
    half = chips * group
    core = lax.rem(lax.axis_index("dp"), 2)

    joined = jnp.concatenate([tokens, cotangent], axis=0)
    slices = jnp.stack([joined[:, d * depth : (d + 1) * depth] for d in range(n_dp)])
    slices = jnp.broadcast_to(slices[:, None], (n_dp, n_tensor, 2 * rows, depth))
    both = lax.all_to_all(
        slices.reshape(n_dp * n_tensor, 2 * rows, depth), ("dp", "tensor"), split_axis=0, concat_axis=0, tiled=True
    )

    def by_core(value):
        value = value.reshape(chips, 2, group, depth)
        value = jnp.where(core == 0, value[:, ::-1], value)
        return value.transpose(1, 0, 2, 3).reshape(2 * half, depth)

    tok, cot = by_core(both[:, :rows]), by_core(both[:, rows:])

    gate_rows, up_rows = gate_weight.T, up_weight.T

    def core_sum(partial):
        got = swap_cores(partial[:half].astype(BF16), n_dp)
        return (partial[half:] + got.astype(F32)).astype(BF16)

    def chip_sum(mine):
        total = mine.astype(F32)
        for shift in range(1, chips):
            got = lax.ppermute(mine, "dp", [(i, (i + 2 * shift) % n_dp) for i in range(n_dp)])
            total = total + got.astype(F32)
        return total

    hid_p = jnp.einsum("td,fd->tf", cot, down_weight, preferred_element_type=F32)
    tok_up, hid_p = lax.optimization_barrier((tok, hid_p))
    up_p = jnp.einsum("td,fd->tf", tok_up, up_rows, preferred_element_type=F32)
    hidden_grad, up = core_sum(hid_p), core_sum(up_p)
    tok_gate, hidden_grad = lax.optimization_barrier((tok, hidden_grad))
    gate_p = jnp.einsum("td,fd->tf", tok_gate, gate_rows, preferred_element_type=F32)
    hidden_grad, up, gate = chip_sum(hidden_grad), chip_sum(up), core_sum(gate_p)

    def both_cores(value):
        return jnp.concatenate([swap_cores(value, n_dp), value], axis=0)

    first = units // 320 * 128
    spans = [slice(0, first), slice(first, units)] if first else [slice(0, units)]
    packed, hidden = [], []
    for span in spans:
        part_gate, part_up, part_hid = chip_sum(gate[:, span]), up[:, span], hidden_grad[:, span]
        sig = jax.nn.sigmoid(part_gate)
        grads = [
            (part_hid * part_up * sig * (1.0 + part_gate * (1.0 - sig))).astype(BF16),
            (part_hid * part_gate * sig).astype(BF16),
        ]
        packed.append(([swap_cores(grad, n_dp) for grad in grads], grads))
        hidden.append((part_gate * sig * part_up).astype(BF16))
    hidden = jnp.concatenate(hidden, axis=1)
    total, parts = None, []
    for span, (other, own) in zip(spans, packed):
        if total is not None:
            total, other = lax.optimization_barrier((total, other))
        parts.append([jnp.concatenate(pair, axis=0) for pair in zip(other, own)])
        part = jnp.einsum("tf,fd->td", parts[-1][0], gate_rows[span], preferred_element_type=F32)
        part = part + jnp.einsum("tf,fd->td", parts[-1][1], up_rows[span], preferred_element_type=F32)
        total = part if total is None else total + part
    gate_grad, up_grad = (jnp.concatenate(values, axis=1) for values in zip(*parts))
    shares = total.astype(BF16).reshape(2, chips, group, depth).transpose(1, 0, 2, 3)
    shares = jnp.where(core == 0, shares[:, ::-1], shares).reshape(n_dp * n_tensor, rows, depth)
    shares, tok, cot, hidden = lax.optimization_barrier((shares, tok, cot, hidden))
    hidden = both_cores(hidden)
    shares = lax.all_to_all(shares, ("dp", "tensor"), split_axis=0, concat_axis=0, tiled=True)
    shares = jnp.sum(shares.astype(F32).reshape(n_dp, n_tensor, rows, depth), axis=1)
    input_grad = shares.transpose(1, 0, 2).reshape(rows, width).astype(BF16)

    grad_gate = (jnp.einsum("td,tf->df", tok, gate_grad, preferred_element_type=F32) / n_dp).astype(BF16)
    grad_up = (jnp.einsum("td,tf->df", tok, up_grad, preferred_element_type=F32) / n_dp).astype(BF16)
    grad_down = (jnp.einsum("tf,td->fd", hidden, cot, preferred_element_type=F32) / n_dp).astype(BF16)
    return (input_grad, grad_gate, grad_up, grad_down)


def solution(mesh):
    return jax.shard_map(
        local,
        mesh=mesh,
        in_specs=(
            P(("dp", "tensor"), None),
            P(("dp", "tensor"), None),
            P("dp", "tensor"),
            P("dp", "tensor"),
            P("tensor", "dp"),
        ),
        out_specs=(
            P(("dp", "tensor"), None),
            P("dp", "tensor"),
            P("dp", "tensor"),
            P("tensor", "dp"),
        ),
        check_vma=False,
    )
```
